32 devices in a mesh: pool: 2 (over y), ctx: 4 (over z), mp: 4 (over x, core).
Axes of the slice: x: 2, y: 2, z: 4, core: 2. Of those that a mesh axis runs over, the one named last changes fastest.
Arguments:
- tokens: bfloat16 [2, 2048, 4096], P('pool', 'ctx', 'mp'), may hold values from -2.5 to 2.5
- norm_gain: float32 [4096], replicated, may hold values from 0.5 to 1.5
- cross_gain: float32 [4096], replicated, may hold values from 0.1 to 1.9
- w_query: bfloat16 [4096, 4096], P(None, 'mp'), may hold values from -8 to 8
- w_key: bfloat16 [4096, 4096], P(None, 'mp'), may hold values from -0.09375 to 0.09375
- w_value: bfloat16 [4096, 4096], P(None, 'mp'), may hold values from -0.09375 to 0.09375
- w_out: bfloat16 [4096, 4096], P('mp'), may hold values from -0.125 to 0.125
- w_cross_query: bfloat16 [4096, 4096], P(None, 'mp'), may hold values from -8 to 8
- w_cross_kv: bfloat16 [2, 896, 4096], P(None, None, 'mp'), may hold values from -0.1875 to 0.1875
- w_cross_out: bfloat16 [4096, 4096], P('mp'), may hold values from -0.125 to 0.125
- encoded: bfloat16 [512, 128, 896], P(('pool', 'ctx'), 'mp'), may hold values from -6 to 6
- owners: int32 [2, 32, 2], replicated, may hold values from 0 to 7, all different within a row; in each aligned block of 8 rows (0 to 7, 8 to 15, ..., all dimensions but the last counted through in order) at most 4 rows name the same one
- slots: int32 [2, 32, 2], replicated, may hold values from 0 to 63
Outputs:
- layer_out: bfloat16 [2, 2048, 4096], P('pool', 'ctx', 'mp')
The draws below stay inside these ranges and needn't reach their ends.
Inputs may be any that keep to these rules, and one draw needn't show every extreme that they name: The 2 neighbours of a span have different owners; among the spans of one index of pool and ctx (aligned blocks of 8 spans, sequence by sequence) no owner is named more than 4 times.
All inputs are finite; a program needn't handle non-finite values.
Results may differ from the reference program's by a relative error of at most 0.035.
Values may be sent and summed in bfloat16 or wider, within the bound.
A program may use at most 192 MiB of HBM per device.

```python
import math
import jax
import jax.numpy as jnp
import numpy as np
from jax import lax

D = 4096
HEADS = 32
HEAD = 128
ENC_W = 896
SPAN = 64
NB_TOK = 128
NB_PER = 2
TOK_DEV = 512
ENC_DEV = 64
SEQS = 2
LEN = 2048
SPANS = 32
SP_DEV = 8
ENC_ROWS = 512
CAP = 4
N_POOL = 2
N_CTX = 4
N_MP = 4


def draw_w_query(key, part):
    key = jax.random.fold_in(key, 11)
    base = jax.random.normal(key, (D, D), jnp.float32)
    factor = jnp.exp(jax.random.uniform(jax.random.fold_in(key, 5), (HEADS,), jnp.float32, 0.0, math.log(2.0)))
    return (base * D ** (-0.5) * jnp.repeat(factor, HEAD)[None, :]).astype(jnp.bfloat16)


def draw_w_cross_query(key, part):
    key = jax.random.fold_in(key, 23)
    base = jax.random.normal(key, (D, D), jnp.float32)
    factor = jnp.exp(jax.random.uniform(jax.random.fold_in(key, 9), (HEADS,), jnp.float32, 0.0, math.log(3.0)))
    return (base * D ** (-0.5) * jnp.repeat(factor, HEAD)[None, :]).astype(jnp.bfloat16)


def touch_ends(drawn, key, smallest, top_value):
    dims = drawn.shape
    index_at = [jax.random.randint(jax.random.fold_in(key, axis), (), 0, dims[axis]) for axis in range(len(dims))]
    drawn = drawn.at[tuple(index_at)].set(smallest)
    longest = dims.index(max(dims))
    index_at[longest] = (index_at[longest] + 1) % dims[longest]
    return drawn.at[tuple(index_at)].set(top_value)


def strengthened(result, stream_key, source, target, blocks, factor):
    owner, partner = [(jnp.arange(result.shape[axis_at]) // (result.shape[axis_at] // blocks)).reshape([-1 if axis == axis_at else 1 for axis in range(result.ndim)]) for axis_at in (source, target)]
    chosen = jax.random.permutation(stream_key, blocks)[partner]
    strong = (owner == chosen) | (owner == (partner + blocks // 2) % blocks)
    return jnp.where(strong, factor * result, result)


def block_scale(rng, extent, split, least, largest):
    factor_of = 1.0
    for axis_at, parts in split:
        draws = jax.random.uniform(jax.random.fold_in(jax.random.fold_in(rng, 6), axis_at), (parts,), jnp.float32, least / len(split), largest / len(split))
        factor_of = factor_of * jnp.repeat(jnp.exp(draws), extent[axis_at] // parts).reshape((-1,) + (1,) * (len(extent) - 1 - axis_at))
    return factor_of


def deal_out(stream_key, own, number, rows, count, top, reach, lean):
    order = jax.random.permutation(stream_key, count)
    heavy_load, usual = portions_of(count, rows * top, reach, lean, True), portions_of(count, rows * top, reach, lean, False)
    places = jnp.arange(count)

    def named(lengths, turn):
        used = int((lengths > 0).sum())
        fixed = max(1, used // 4)
        passed = fixed + (places - fixed + turn * (used - fixed)) % max(1, count - fixed)
        return jnp.zeros((count,), jnp.int32).at[order[jnp.where(places < fixed, places, passed)]].set(jnp.asarray(lengths, jnp.int32))

    lengths = jnp.where(number % 4 == 0, named(heavy_load, number // 4), named(usual, number - number // 4 - 1))
    mixed = jax.random.permutation(jax.random.fold_in(own, 3), count)
    donor, taker = mixed[0:count // 2 * 2:2], mixed[1:count // 2 * 2:2]
    room = jnp.minimum(lengths[donor] - 1, reach - lengths[taker]) // 2
    room = jnp.where((donor == order[0]) | (taker == order[0]) | (lengths[taker] == 0), 0, jnp.maximum(room, 0))
    passed = jax.random.randint(jax.random.fold_in(own, 4), (count // 2,), 0, 1 << 20) % (room + 1)
    lengths = lengths.at[donor].add(-passed).at[taker].add(passed)
    members = jnp.searchsorted(jnp.cumsum(lengths), jnp.arange(rows * top), side="right").astype(jnp.int32)
    table = members.reshape(top, rows).T
    table = table[jax.random.permutation(jax.random.fold_in(own, 1), rows)]
    turn = jax.random.randint(jax.random.fold_in(own, 2), (rows, 1), 0, top)
    return jnp.take_along_axis(table, (jnp.arange(top)[None, :] + turn) % top, axis=1)


def portions_of(count, total, limit, skew, full):
    loads = [(1 << 20) // math.isqrt(rank ** skew) + 1 for rank in range(1, count + 1)]
    largest = limit if full else min(limit, max(-(-total // count), total * loads[0] // sum(loads)))
    least = 1 if total - largest >= count - 1 else 0
    counts, spare = [largest] + [least] * (count - 1), total - largest - least * (count - 1)
    while spare > 0:
        candidates = [i for i in range(1, count) if counts[i] < largest] or [i for i in range(1, count) if counts[i] < limit]
        mass, left = sum([loads[i] for i in candidates]), spare
        for i in candidates:
            addition = min(limit - counts[i], max(1, left * loads[i] // mass), spare)
            counts[i] = counts[i] + addition
            spare = spare - addition
    return np.array(counts)


def noise(key, dims, scale, most, split=(), kind=jnp.bfloat16):
    gain = block_scale(key, dims, split, -0.22, 0.18) if split else 1.0
    drawn = jax.random.normal(key, dims, jnp.float32) * scale * gain
    return jnp.minimum(jnp.maximum(drawn, -most), most).astype(kind)


def heavy_noise(stream_key, shape, spread, bound, pieces, heavy, held_as=jnp.bfloat16):
    drawn = spread * jax.random.normal(stream_key, shape, jnp.float32)
    if pieces:
        drawn = drawn * block_scale(stream_key, shape, pieces, -0.22, 0.18)
    return jnp.clip(strengthened(drawn, jax.random.fold_in(stream_key, 3), *heavy), -bound, bound).astype(held_as)


def setup_inputs(seed: int = 0) -> dict:
    arg_keys = jax.random.split(jax.random.key(seed), 14)
    tokens = noise(arg_keys[0], (SEQS, LEN, D), 0.4, 2.5, ((0, 2), (1, 4), (2, 4)))
    norm_gain = jnp.clip(1.0 + 0.1 * jax.random.normal(arg_keys[1], (D,), jnp.float32), 0.5, 1.5)
    cross_gain = jnp.clip(1.0 + 0.18 * jax.random.normal(arg_keys[2], (D,), jnp.float32), 0.1, 1.9)
    w_query = draw_w_query(jax.random.fold_in(arg_keys[13], 71), 0)
    w_key = noise(arg_keys[4], (D, D), D ** -0.5, 0.09375, ((1, 4),))
    w_value = noise(arg_keys[5], (D, D), D ** -0.5, 0.09375, ((1, 4),))
    w_out = heavy_noise(arg_keys[6], (D, D), D ** -0.5, 0.125, ((0, 4),), (0, 1, 4, 2.0))
    w_cross_query = draw_w_cross_query(jax.random.fold_in(arg_keys[13], 71), 0)
    w_cross_kv = noise(arg_keys[8], (2, ENC_W, D), ENC_W ** -0.5, 0.1875, ((2, 4),))
    w_cross_out = heavy_noise(arg_keys[9], (D, D), D ** -0.5, 0.125, ((0, 4),), (0, 1, 4, 2.0))
    encoded = noise(arg_keys[10], (ENC_ROWS, NB_TOK, ENC_W), 1.0, 6.0, ((0, 8), (1, 4)))
    owners_keys = jax.random.split(jax.random.fold_in(arg_keys[11], 1), SEQS * SPANS // SP_DEV)
    owners_turns = jax.random.permutation(jax.random.fold_in(arg_keys[11], 3), SEQS * SPANS // SP_DEV)
    owners = jax.vmap(lambda own, number: deal_out(jax.random.fold_in(arg_keys[11], 2), own, number, SP_DEV, N_POOL * N_CTX, NB_PER, CAP, 2))(owners_keys, owners_turns).reshape((SEQS, SPANS, NB_PER))
    slots = touch_ends(jax.random.randint(arg_keys[12], (SEQS, SPANS, NB_PER), 0, ENC_DEV), jax.random.fold_in(arg_keys[12], 1), 0, ENC_DEV - 1).astype(jnp.int32)
    return {"tokens": tokens, "norm_gain": norm_gain, "cross_gain": cross_gain, "w_query": w_query, "w_key": w_key, "w_value": w_value, "w_out": w_out, "w_cross_query": w_cross_query, "w_cross_kv": w_cross_kv, "w_cross_out": w_cross_out, "encoded": encoded, "owners": owners, "slots": slots}


norm_eps = 1e-05

def rms_scaled(inputs, gain_vector):
    floats = inputs.astype(jnp.float32)
    return floats * lax.rsqrt(lax.optimization_barrier(jnp.mean(floats * floats, axis=-1, keepdims=True)) + norm_eps) * gain_vector.astype(jnp.float32)

def split_sum(inputs, weight):
    group_width = inputs.shape[1] // N_MP

    def add_group(running, group_index):
        left_part = lax.dynamic_slice_in_dim(inputs, group_index * group_width, group_width, 1)
        right_part = lax.dynamic_slice_in_dim(weight, group_index * group_width, group_width, 0)
        partial_sum = jnp.dot(left_part, right_part, preferred_element_type=jnp.float32).astype(jnp.bfloat16)
        partial_sum = lax.optimization_barrier(partial_sum)
        return (running + partial_sum.astype(jnp.float32), None)
    start_sum = jnp.zeros((inputs.shape[0], weight.shape[1]), jnp.float32)
    summed, unused = lax.scan(add_group, start_sum, jnp.arange(N_MP, dtype=jnp.int32))
    return summed

def self_attend(queries, keys_all, values_all):
    score_scale = HEAD ** (-0.5)
    key_pos = jnp.arange(LEN, dtype=jnp.int32)

    def one_block(block_index):
        block_queries = lax.dynamic_slice_in_dim(queries, block_index * TOK_DEV, TOK_DEV, 0)
        scores = jnp.einsum('qhe,khe->hqk', block_queries.astype(jnp.float32), keys_all.astype(jnp.float32)) * score_scale
        query_pos = block_index * TOK_DEV + jnp.arange(TOK_DEV, dtype=jnp.int32)
        allowed = key_pos[None, :] <= query_pos[:, None]
        scores = jnp.where(allowed[None], scores, -jnp.inf)
        peak = lax.optimization_barrier(jnp.max(scores, axis=-1, keepdims=True))
        weights = jnp.exp(scores - peak)
        totals = lax.optimization_barrier(jnp.sum(weights, axis=-1))
        rounded = lax.optimization_barrier(weights.astype(jnp.bfloat16))
        mixed_out = jnp.einsum('hqk,khe->qhe', rounded.astype(jnp.float32), values_all.astype(jnp.float32))
        return (mixed_out / jnp.transpose(totals)[:, :, None]).astype(jnp.bfloat16)
    blocks = lax.map(one_block, jnp.arange(N_CTX, dtype=jnp.int32))
    return blocks.reshape(LEN, HEADS * HEAD)

def cross_attend(queries, keys_nb, values_nb):
    score_scale = HEAD ** (-0.5)
    lag_rows = SPAN - 1
    shifted = jnp.concatenate([queries[lag_rows:], jnp.zeros((lag_rows, HEADS, HEAD), jnp.bfloat16)], axis=0)
    shifted = shifted.reshape(SPANS, SPAN, HEADS, HEAD)
    keys_flat = keys_nb.reshape(SPANS, NB_PER * NB_TOK, HEADS, HEAD)
    values_flat = values_nb.reshape(SPANS, NB_PER * NB_TOK, HEADS, HEAD)
    scores = jnp.einsum('cmhe,cnhe->chmn', shifted.astype(jnp.float32), keys_flat.astype(jnp.float32)) * score_scale
    peak = lax.optimization_barrier(jnp.max(scores, axis=-1, keepdims=True))
    weights = jnp.exp(scores - peak)
    totals = lax.optimization_barrier(jnp.sum(weights, axis=-1))
    rounded = lax.optimization_barrier(weights.astype(jnp.bfloat16))
    mixed_out = jnp.einsum('chmn,cnhe->cmhe', rounded.astype(jnp.float32), values_flat.astype(jnp.float32))
    mixed_out = (mixed_out / jnp.transpose(totals, (0, 2, 1))[..., None]).astype(jnp.bfloat16)
    mixed_out = mixed_out.reshape(LEN, HEADS * HEAD)
    return jnp.concatenate([jnp.zeros((lag_rows, HEADS * HEAD), jnp.bfloat16), mixed_out[:LEN - lag_rows]], axis=0)

def reference(tokens, norm_gain, cross_gain, w_query, w_key, w_value, w_out, w_cross_query, w_cross_kv, w_cross_out, encoded, owners, slots):
    results = []
    for seq_index in range(SEQS):
        seq_tokens = tokens[seq_index]
        normed = rms_scaled(seq_tokens, norm_gain).astype(jnp.bfloat16)
        queries = jnp.dot(normed, w_query, preferred_element_type=jnp.float32).astype(jnp.bfloat16).reshape(LEN, HEADS, HEAD)
        keys_all = jnp.dot(normed, w_key, preferred_element_type=jnp.float32).astype(jnp.bfloat16).reshape(LEN, HEADS, HEAD)
        values_all = jnp.dot(normed, w_value, preferred_element_type=jnp.float32).astype(jnp.bfloat16).reshape(LEN, HEADS, HEAD)
        attended = self_attend(queries, keys_all, values_all)
        mixed = (seq_tokens.astype(jnp.float32) + split_sum(attended, w_out)).astype(jnp.bfloat16)
        cross_in = rms_scaled(mixed, cross_gain).astype(jnp.bfloat16)
        cross_queries = jnp.dot(cross_in, w_cross_query, preferred_element_type=jnp.float32).astype(jnp.bfloat16).reshape(LEN, HEADS, HEAD)
        row_ids = (owners[seq_index] * ENC_DEV + slots[seq_index]).reshape(-1).astype(jnp.int32)
        fetched = encoded[row_ids].astype(jnp.float32)
        keys_nb = jnp.einsum('nrw,wd->nrd', fetched, w_cross_kv[0].astype(jnp.float32)).astype(jnp.bfloat16)
        values_nb = jnp.einsum('nrw,wd->nrd', fetched, w_cross_kv[1].astype(jnp.float32)).astype(jnp.bfloat16)
        keys_nb = keys_nb.reshape(SPANS, NB_PER, NB_TOK, HEADS, HEAD)
        values_nb = values_nb.reshape(SPANS, NB_PER, NB_TOK, HEADS, HEAD)
        crossed = cross_attend(cross_queries, keys_nb, values_nb)
        results.append((mixed.astype(jnp.float32) + split_sum(crossed, w_cross_out)).astype(jnp.bfloat16))
    return jnp.stack(results)
```

```python
import functools

import jax
import jax.numpy as jnp
from jax import lax
from jax.experimental import pallas as pl
from jax.experimental.pallas import tpu as pltpu
from jax.sharding import PartitionSpec as P

HEAD = 128
SPAN = 64
NB_TOK = 128
NB_PER = 2
MIB = 1 << 20
LOG2E = 1.4426950408889634

norm_eps = 1e-05


def params(mib, steps=1):
    return pltpu.CompilerParams(
        vmem_limit_bytes=mib * MIB, dimension_semantics=("arbitrary",) * steps
    )


def cost(flops, moved, exps=0):
    return pl.CostEstimate(flops=int(flops), bytes_accessed=int(moved), transcendentals=int(exps))


def from_behind(block, axis, distance):
    devices = range(lax.axis_size(axis))
    route = [(i - distance, i) for i in devices if i - distance in devices]
    return lax.ppermute(block, axis, route)


def swap(block, bit):
    return lax.ppermute(block, "mp", [(i, i ^ bit) for i in range(lax.axis_size("mp"))])


def gather_blocks(block):
    count = lax.axis_size("mp")
    blocks = {0: block}
    bit = count // 2
    while bit:
        blocks.update({o ^ bit: swap(b, bit) for o, b in list(blocks.items())})
        bit //= 2
    return [blocks[o] for o in range(count)]


def scatter_sum(partials):
    count = lax.axis_size("mp")
    held = dict(enumerate(partials))
    bit = 1
    while bit < count:
        summed = {}
        for o in sorted((o for o in held if not o & bit), reverse=True):
            total = held[o].astype(jnp.float32) + swap(held[o | bit], bit).astype(jnp.float32)
            summed[o] = total if 2 * bit == count else total.astype(jnp.bfloat16)
        held = summed
        bit *= 2
    return held[0]


def norm_kernel(place_ref, gain_ref, *refs):
    *blocks, out_ref = refs
    width = blocks[0].shape[1]
    features = width * len(blocks)
    squares = 0.0
    for b in blocks:
        x = b[...].astype(jnp.float32)
        squares += jnp.sum(x * x, axis=1, keepdims=True)
    scale = lax.rsqrt(squares / features + norm_eps)
    for o, b in enumerate(blocks):
        columns = pl.ds(pl.multiple_of(place_ref[o] * width, width), width)
        out_ref[:, columns] = (b[...].astype(jnp.float32) * scale * gain_ref[:, columns]).astype(
            jnp.bfloat16
        )


def normalised(blocks, gain):
    rows, width = blocks[0].shape
    features = width * len(blocks)
    tile = min(rows, 128)
    places = lax.axis_index("mp") ^ jnp.arange(len(blocks), dtype=jnp.int32)
    return pl.pallas_call(
        norm_kernel,
        grid_spec=pltpu.PrefetchScalarGridSpec(
            num_scalar_prefetch=1,
            grid=(rows // tile,),
            in_specs=[pl.BlockSpec((1, features), lambda i, p: (0, 0))]
            + [pl.BlockSpec((tile, width), lambda i, p: (i, 0))] * len(blocks),
            out_specs=pl.BlockSpec((tile, features), lambda i, p: (i, 0)),
        ),
        out_shape=jax.ShapeDtypeStruct((rows, features), jnp.bfloat16),
        compiler_params=params(24),
        cost_estimate=cost(6 * rows * features, 4 * rows * features),
        name="norm",
    )(places, gain.reshape(1, features), *blocks)


def project_kernel(flip, x_ref, w_ref, out_ref):
    product = jnp.dot(x_ref[...], w_ref[...], preferred_element_type=jnp.float32)
    if flip:
        product = jnp.transpose(product)
    out_ref[...] = product.astype(jnp.bfloat16)


def project(x, w, first, width, flip=False):
    rows, depth = x.shape
    tile = min(width, 256)
    base = first // tile
    if flip:
        out_spec, out_dims = pl.BlockSpec((tile, rows), lambda j: (j, 0)), (width, rows)
    else:
        out_spec, out_dims = pl.BlockSpec((rows, tile), lambda j: (0, j)), (rows, width)
    return pl.pallas_call(
        functools.partial(project_kernel, flip),
        grid=(width // tile,),
        in_specs=[
            pl.BlockSpec((rows, depth), lambda j: (0, 0)),
            pl.BlockSpec((depth, tile), lambda j: (0, base + j)),
        ],
        out_specs=out_spec,
        out_shape=jax.ShapeDtypeStruct(out_dims, jnp.bfloat16),
        compiler_params=params(24),
        cost_estimate=cost(2 * rows * depth * width, 2 * depth * (rows + width)),
        name="project",
    )(x, w)


def block_kernel(place_ref, x_ref, w_ref, out_ref):
    out_ref[...] = jnp.dot(
        x_ref[...], w_ref[...], preferred_element_type=jnp.float32
    ).astype(jnp.bfloat16)


def project_block(x, w, place, width):
    rows, depth = x.shape
    tile = min(width, 512)
    steps = width // tile
    return pl.pallas_call(
        block_kernel,
        grid_spec=pltpu.PrefetchScalarGridSpec(
            num_scalar_prefetch=1,
            grid=(steps,),
            in_specs=[
                pl.BlockSpec((rows, depth), lambda j, p: (0, 0)),
                pl.BlockSpec((depth, tile), lambda j, p: (0, p[0] * steps + j)),
            ],
            out_specs=pl.BlockSpec((rows, tile), lambda j, p: (0, j)),
        ),
        out_shape=jax.ShapeDtypeStruct((rows, width), jnp.bfloat16),
        compiler_params=params(16),
        cost_estimate=cost(2 * rows * depth * width, 2 * depth * (rows + width)),
        name="project_block",
    )(place.reshape(1), x, w)


def project_scattered(x, w):
    count = lax.axis_size("mp")
    width = w.shape[1] // count
    me = lax.axis_index("mp")
    partials = {}
    for o in sorted(range(count), key=lambda o: (1 - o % 2, -o)):
        partials[o] = project_block(x, w, me ^ o, width)
    return scatter_sum([partials[o] for o in range(count)])


def scores_of(keys, queries):
    return lax.dot_general(
        keys, queries, (((1,), (1,)), ((), ())), preferred_element_type=jnp.float32
    ) * (HEAD**-0.5 * LOG2E)


def attend(parts):
    peak = functools.reduce(jnp.maximum, [jnp.max(s, axis=0, keepdims=True) for s, _ in parts])
    total, out = 0.0, 0.0
    for s, values in parts:
        weights = jnp.exp2(s - peak)
        total += jnp.sum(weights, axis=0, keepdims=True)
        out += jnp.dot(values, weights.astype(jnp.bfloat16), preferred_element_type=jnp.float32)
    return out / total, peak + jnp.log2(total)


def far_kernel(flag_ref, qa, qb, k0, v0, k1, v1, oa, la, ob, lb):
    rows = qa.shape[0]
    tile = min(rows, 256)

    @pl.when(flag_ref[0] == 1)
    def _():
        for q, o, l in ((qa, oa, la), (qb, ob, lb)):
            for at in range(0, rows, tile):
                queries = q[at : at + tile, :]
                out, log = attend(
                    [(scores_of(k0[...], queries), v0[...]), (scores_of(k1[...], queries), v1[...])]
                )
                o[:, at : at + tile] = out.astype(jnp.bfloat16)
                l[0, :, at : at + tile] = log


def near_kernel(flag_ref, q, k0, v0, k1, v1, o, l):
    rows = q.shape[0]
    tile = min(rows, 256)

    def run(with_earlier):
        for at in range(0, rows, tile):
            queries = q[at : at + tile, :]
            end = at + tile
            own = scores_of(k1[:end, :], queries)
            key_pos = lax.broadcasted_iota(jnp.int32, own.shape, 0)
            query_pos = at + lax.broadcasted_iota(jnp.int32, own.shape, 1)
            own = jnp.where(key_pos <= query_pos, own, -1e30)
            parts = [(own, v1[:, :end])]
            if with_earlier:
                parts.append((scores_of(k0[...], queries), v0[...]))
            out, log = attend(parts)
            o[:, at:end] = out.astype(jnp.bfloat16)
            l[0, :, at:end] = log

    @pl.when(flag_ref[0] % 2 == 1)
    def _():
        run(True)

    @pl.when(flag_ref[0] % 2 == 0)
    def _():
        run(False)


def merge_kernel(flag_ref, o, l, far_o, far_l, out):
    @pl.when(flag_ref[0] >= 2)
    def _():
        peak = jnp.maximum(l[0], far_l[0])
        here, there = jnp.exp2(l[0] - peak), jnp.exp2(far_l[0] - peak)
        mixed = (o[...].astype(jnp.float32) * here + far_o[...].astype(jnp.float32) * there) / (
            here + there
        )
        out[...] = jnp.transpose(mixed).astype(jnp.bfloat16)

    @pl.when(flag_ref[0] < 2)
    def _():
        out[...] = jnp.transpose(o[...].astype(jnp.float32)).astype(jnp.bfloat16)


def head_call(kernel, name, flag, rows, heads, ins, outs, work):
    specs = {
        "rows": (pl.BlockSpec((rows, HEAD), lambda h, f: (0, h)), (rows, heads * HEAD), jnp.bfloat16),
        "flat": (pl.BlockSpec((HEAD, rows), lambda h, f: (h, 0)), (heads * HEAD, rows), jnp.bfloat16),
        "log": (pl.BlockSpec((1, 1, rows), lambda h, f: (h, 0, 0)), (heads, 1, rows), jnp.float32),
    }
    return pl.pallas_call(
        kernel,
        grid_spec=pltpu.PrefetchScalarGridSpec(
            num_scalar_prefetch=1,
            grid=(heads,),
            in_specs=[specs[kind][0] for kind, _ in ins],
            out_specs=[specs[kind][0] for kind in outs],
        ),
        out_shape=[jax.ShapeDtypeStruct(specs[kind][1], specs[kind][2]) for kind in outs],
        compiler_params=params(24),
        cost_estimate=cost(
            4 * HEAD * work * heads, 2 * rows * HEAD * heads * len(ins), work * heads
        ),
        name=name,
    )(flag, *[x for _, x in ins])


def self_attention(normed, w_query, w_key, w_value):
    rows = normed.shape[0]
    assert lax.axis_size("ctx") == 4
    ctx = lax.axis_index("ctx")
    width = w_query.shape[1] // 2
    heads = width // HEAD
    flag = ctx.reshape(1)
    merged = []
    for first in (0, width):
        q = project(normed, w_query, first, width)
        qa = lax.ppermute(q, "ctx", [(2, 1)])
        qb = lax.ppermute(q, "ctx", [(3, 1)])
        k = project(normed, w_key, first, width)
        k0 = lax.ppermute(k, "ctx", [(0, 1), (2, 3)])
        v = project(normed, w_value, first, width, flip=True)
        v0 = lax.ppermute(v, "ctx", [(0, 1), (2, 3)])
        keys = [("rows", k0), ("flat", v0), ("rows", k), ("flat", v)]
        oa, la, ob, lb = head_call(
            far_kernel, "far_attention", flag, rows, heads,
            [("rows", qa), ("rows", qb)] + keys, ["flat", "log"] * 2, 4 * rows * rows,
        )
        far_a = [lax.ppermute(x, "ctx", [(1, 2)]) for x in (oa, la)]
        far_b = [lax.ppermute(x, "ctx", [(1, 3)]) for x in (ob, lb)]
        o, l = head_call(
            near_kernel, "near_attention", flag, rows, heads,
            [("rows", q)] + keys, ["flat", "log"], 2 * rows * rows,
        )
        far_o, far_l = [jnp.where(ctx == 3, b, a) for a, b in zip(far_a, far_b)]
        (out,) = head_call(
            merge_kernel, "merge", flag, rows, heads,
            [("flat", o), ("log", l), ("flat", far_o), ("log", far_l)], ["rows"], rows,
        )
        merged.append(out)
    return jnp.concatenate(merged, axis=1)


def fetch_neighbours(encoded, owners, slots):
    group_count = lax.axis_size(("pool", "ctx"))
    my_group = lax.axis_index(("pool", "ctx"))
    per_group = owners.size // group_count
    capacity = max(2, 2 * per_group // group_count)
    owner_table = owners.reshape(group_count, per_group)
    slot_table = slots.reshape(group_count, per_group)
    matched = (owner_table == my_group).astype(jnp.int32)
    order_rank = jnp.cumsum(matched, axis=1) - 1
    slot_index = jnp.arange(capacity, dtype=jnp.int32)
    picked = matched[:, None, :] * (order_rank[:, None, :] == slot_index[None, :, None]).astype(
        jnp.int32
    )
    source_rows = jnp.sum(picked * slot_table[:, None, :], axis=2).reshape(-1)
    outgoing = encoded[source_rows].reshape((group_count, capacity) + encoded.shape[1:])
    incoming = lax.all_to_all(outgoing, ("pool", "ctx"), split_axis=0, concat_axis=0, tiled=True)
    wanted = lax.dynamic_index_in_dim(owner_table, my_group, 0, keepdims=False)
    positions = jnp.arange(per_group, dtype=jnp.int32)
    same_owner = (wanted[:, None] == wanted[None, :]).astype(jnp.int32)
    before_this = (positions[None, :] < positions[:, None]).astype(jnp.int32)
    arrival = wanted * capacity + jnp.sum(same_owner * before_this, axis=1)
    arrived = incoming.reshape((group_count * capacity,) + encoded.shape[1:])[arrival]
    earlier = from_behind(arrived[-NB_PER:], "ctx", 1)
    extended = jnp.concatenate([earlier, arrived], axis=0)
    return lax.all_gather(extended, "mp", axis=1, tiled=True)


def neighbour_kernel(x_ref, w_ref, out_ref):
    out_ref[0] = jnp.dot(x_ref[...], w_ref[0], preferred_element_type=jnp.float32).astype(
        jnp.bfloat16
    )


def neighbour_kv(fetched, w_cross_kv):
    rows, depth = fetched.shape[0] * fetched.shape[1], fetched.shape[2]
    width = w_cross_kv.shape[2]
    tile = min(width, 256)
    steps = width // tile
    return pl.pallas_call(
        neighbour_kernel,
        grid=(2, steps),
        in_specs=[
            pl.BlockSpec((rows, depth), lambda c, j: (0, 0)),
            pl.BlockSpec((1, depth, tile), lambda c, j: (c, 0, j)),
        ],
        out_specs=pl.BlockSpec((1, rows, tile), lambda c, j: (c, 0, j)),
        out_shape=jax.ShapeDtypeStruct((2, rows, width), jnp.bfloat16),
        compiler_params=params(32, 2),
        cost_estimate=cost(4 * rows * depth * width, 4 * rows * width + 2 * rows * depth),
        name="neighbour_kv",
    )(fetched.reshape(rows, depth), w_cross_kv)


def cross_kernel(q_ref, k_ref, v_ref, out_ref):
    rows = q_ref.shape[0]
    named = NB_PER * NB_TOK
    spans = rows // SPAN
    queries = pltpu.roll(q_ref[...].astype(jnp.float32), 1, 0).astype(jnp.bfloat16)

    def one(part, span):
        keys = k_ref[0, span * named : (span + 1) * named, :]
        values = v_ref[0, span * named : (span + 1) * named, :]
        s = lax.dot_general(
            part, keys, (((1,), (1,)), ((), ())), preferred_element_type=jnp.float32
        ) * (HEAD**-0.5 * LOG2E)
        weights = jnp.exp2(s - jnp.max(s, axis=1, keepdims=True))
        total = jnp.sum(weights, axis=1, keepdims=True)
        out = jnp.dot(weights.astype(jnp.bfloat16), values, preferred_element_type=jnp.float32)
        return out / total

    outs = [one(queries[c * SPAN : (c + 1) * SPAN], c) for c in range(spans)]
    last = one(queries[:16], spans)
    whole = jnp.concatenate(outs, axis=0)
    last_row = jnp.broadcast_to(last[:1], whole.shape)
    row = lax.broadcasted_iota(jnp.int32, whole.shape, 0)
    whole = jnp.where(row == 0, last_row, whole)
    out_ref[...] = pltpu.roll(whole, rows - 1, 0).astype(jnp.bfloat16)


def cross_attention(queries, kv):
    rows, width = queries.shape
    heads = width // HEAD
    return pl.pallas_call(
        cross_kernel,
        grid=(heads,),
        in_specs=[
            pl.BlockSpec((rows, HEAD), lambda h: (0, h)),
            pl.BlockSpec((1, kv.shape[1], HEAD), lambda h: (0, 0, h)),
            pl.BlockSpec((1, kv.shape[1], HEAD), lambda h: (1, 0, h)),
        ],
        out_specs=pl.BlockSpec((rows, HEAD), lambda h: (0, h)),
        out_shape=jax.ShapeDtypeStruct((rows, width), jnp.bfloat16),
        compiler_params=params(24),
        cost_estimate=cost(1024 * rows * width, 4 * kv.shape[1] * width, 2 * rows * width),
        name="cross_attention",
    )(queries, kv, kv)


def per_device(
    tokens,
    norm_gain,
    cross_gain,
    w_query,
    w_key,
    w_value,
    w_out,
    w_cross_query,
    w_cross_kv,
    w_cross_out,
    encoded,
    owners,
    slots,
):
    own = tokens[0]
    normed = normalised(gather_blocks(own), norm_gain)
    fetched = fetch_neighbours(encoded, owners, slots)
    attended = self_attention(normed, w_query, w_key, w_value)
    kv = neighbour_kv(fetched, w_cross_kv)
    share = project_scattered(attended, w_out)
    residual = (own.astype(jnp.float32) + share).astype(jnp.bfloat16)
    cross_in = normalised(gather_blocks(residual), cross_gain)
    cross_queries = project(cross_in, w_cross_query, 0, w_cross_query.shape[1])
    crossed = cross_attention(cross_queries, kv)
    cross_part = project_scattered(crossed, w_cross_out)
    return (residual.astype(jnp.float32) + cross_part).astype(jnp.bfloat16)[None]


def solution(mesh):
    placed = (
        P("pool", "ctx", "mp"),
        P(),
        P(),
        P(None, "mp"),
        P(None, "mp"),
        P(None, "mp"),
        P("mp", None),
        P(None, "mp"),
        P(None, None, "mp"),
        P("mp", None),
        P(("pool", "ctx"), "mp", None),
        P(),
        P(),
    )
    return jax.shard_map(
        per_device, mesh=mesh, in_specs=placed, out_specs=P("pool", "ctx", "mp"), check_vma=False
    )
```

```python
import functools

import jax
import jax.numpy as jnp
from jax import lax
from jax.experimental import pallas as pl
from jax.experimental.pallas import tpu as pltpu
from jax.sharding import PartitionSpec as P

HEAD = 128
SPAN = 64
NB_TOK = 128
NB_PER = 2
MIB = 1 << 20
LOG2E = 1.4426950408889634

norm_eps = 1e-05


def params(mib, steps=1):
    return pltpu.CompilerParams(
        vmem_limit_bytes=mib * MIB, dimension_semantics=("arbitrary",) * steps
    )


def cost(flops, moved, exps=0):
    return pl.CostEstimate(flops=int(flops), bytes_accessed=int(moved), transcendentals=int(exps))


def in_hbm(weight):
    return pltpu.with_memory_space_constraint(weight, pltpu.HBM)


def from_behind(block, axis, distance):
    devices = range(lax.axis_size(axis))
    route = [(i - distance, i) for i in devices if i - distance in devices]
    return lax.ppermute(block, axis, route)


def swap(block, bit):
    return lax.ppermute(block, "mp", [(i, i ^ bit) for i in range(lax.axis_size("mp"))])


def gather_blocks(block):
    count = lax.axis_size("mp")
    blocks = {0: block}
    bit = count // 2
    while bit:
        blocks.update({o ^ bit: swap(b, bit) for o, b in list(blocks.items())})
        bit //= 2
    return [blocks[o] for o in range(count)]


def scatter_sum(partials):
    count = lax.axis_size("mp")
    held = dict(enumerate(partials))
    bit = 1
    while bit < count:
        summed = {}
        for o in sorted((o for o in held if not o & bit), reverse=True):
            total = held[o].astype(jnp.float32) + swap(held[o | bit], bit).astype(jnp.float32)
            summed[o] = total if 2 * bit == count else total.astype(jnp.bfloat16)
        held = summed
        bit *= 2
    return held[0]


def norm_kernel(place_ref, gain_ref, *refs):
    *blocks, out_ref = refs
    width = blocks[0].shape[1]
    features = width * len(blocks)
    squares = 0.0
    for b in blocks:
        x = b[...].astype(jnp.float32)
        squares += jnp.sum(x * x, axis=1, keepdims=True)
    scale = lax.rsqrt(squares / features + norm_eps)
    for o, b in enumerate(blocks):
        columns = pl.ds(pl.multiple_of(place_ref[o] * width, width), width)
        out_ref[:, columns] = (b[...].astype(jnp.float32) * scale * gain_ref[:, columns]).astype(
            jnp.bfloat16
        )


def normalised(blocks, gain):
    rows, width = blocks[0].shape
    features = width * len(blocks)
    tile = min(rows, 128)
    places = lax.axis_index("mp") ^ jnp.arange(len(blocks), dtype=jnp.int32)
    return pl.pallas_call(
        norm_kernel,
        grid_spec=pltpu.PrefetchScalarGridSpec(
            num_scalar_prefetch=1,
            grid=(rows // tile,),
            in_specs=[pl.BlockSpec((1, features), lambda i, p: (0, 0))]
            + [pl.BlockSpec((tile, width), lambda i, p: (i, 0))] * len(blocks),
            out_specs=pl.BlockSpec((tile, features), lambda i, p: (i, 0)),
        ),
        out_shape=jax.ShapeDtypeStruct((rows, features), jnp.bfloat16),
        compiler_params=params(24),
        cost_estimate=cost(6 * rows * features, 4 * rows * features),
        name="norm",
    )(places, gain.reshape(1, features), *blocks)


def project_kernel(flip, x_ref, w_ref, out_ref):
    product = jnp.dot(x_ref[...], w_ref[...], preferred_element_type=jnp.float32)
    if flip:
        product = jnp.transpose(product)
    out_ref[...] = product.astype(jnp.bfloat16)


def project(x, w, first, width, flip=False):
    rows, depth = x.shape
    tile = min(width, 256)
    base = first // tile
    if flip:
        out_spec, out_dims = pl.BlockSpec((tile, rows), lambda j: (j, 0)), (width, rows)
    else:
        out_spec, out_dims = pl.BlockSpec((rows, tile), lambda j: (0, j)), (rows, width)
    return pl.pallas_call(
        functools.partial(project_kernel, flip),
        grid=(width // tile,),
        in_specs=[
            pl.BlockSpec((rows, depth), lambda j: (0, 0)),
            pl.BlockSpec((depth, tile), lambda j: (0, base + j)),
        ],
        out_specs=out_spec,
        out_shape=jax.ShapeDtypeStruct(out_dims, jnp.bfloat16),
        compiler_params=params(24),
        cost_estimate=cost(2 * rows * depth * width, 2 * depth * (rows + width)),
        name="project",
    )(x, in_hbm(w))


def block_kernel(place_ref, x_ref, w_ref, out_ref):
    out_ref[...] = jnp.dot(
        x_ref[...], w_ref[...], preferred_element_type=jnp.float32
    ).astype(jnp.bfloat16)


def project_block(x, w, place, width):
    rows, depth = x.shape
    tile = min(width, 512)
    steps = width // tile
    return pl.pallas_call(
        block_kernel,
        grid_spec=pltpu.PrefetchScalarGridSpec(
            num_scalar_prefetch=1,
            grid=(steps,),
            in_specs=[
                pl.BlockSpec((rows, depth), lambda j, p: (0, 0)),
                pl.BlockSpec((depth, tile), lambda j, p: (0, p[0] * steps + j)),
            ],
            out_specs=pl.BlockSpec((rows, tile), lambda j, p: (0, j)),
        ),
        out_shape=jax.ShapeDtypeStruct((rows, width), jnp.bfloat16),
        compiler_params=params(16),
        cost_estimate=cost(2 * rows * depth * width, 2 * depth * (rows + width)),
        name="project_block",
    )(place.reshape(1), x, in_hbm(w))


def project_scattered(x, w):
    count = lax.axis_size("mp")
    width = w.shape[1] // count
    me = lax.axis_index("mp")
    partials = {}
    for o in sorted(range(count), key=lambda o: (1 - o % 2, -o)):
        partials[o] = project_block(x, w, me ^ o, width)
    return scatter_sum([partials[o] for o in range(count)])


def scores_of(keys, queries):
    return lax.dot_general(
        keys, queries, (((1,), (1,)), ((), ())), preferred_element_type=jnp.float32
    ) * (HEAD**-0.5 * LOG2E)


def attend(parts):
    peak = functools.reduce(jnp.maximum, [jnp.max(s, axis=0, keepdims=True) for s, _ in parts])
    total, out = 0.0, 0.0
    for s, values in parts:
        weights = jnp.exp2(s - peak)
        total += jnp.sum(weights, axis=0, keepdims=True)
        out += jnp.dot(values, weights.astype(jnp.bfloat16), preferred_element_type=jnp.float32)
    return out / total, peak + jnp.log2(total)


def far_kernel(flag_ref, qa, qb, k0, v0, k1, v1, oa, la, ob, lb):
    rows = qa.shape[0]
    tile = min(rows, 256)

    @pl.when(flag_ref[0] == 1)
    def _():
        for q, o, l in ((qa, oa, la), (qb, ob, lb)):
            for at in range(0, rows, tile):
                queries = q[at : at + tile, :]
                out, log = attend(
                    [(scores_of(k0[...], queries), v0[...]), (scores_of(k1[...], queries), v1[...])]
                )
                o[:, at : at + tile] = out.astype(jnp.bfloat16)
                l[0, :, at : at + tile] = log


def near_kernel(flag_ref, q, k0, v0, k1, v1, o, l):
    rows = q.shape[0]
    tile = min(rows, 256)

    def run(with_earlier):
        for at in range(0, rows, tile):
            queries = q[at : at + tile, :]
            end = at + tile
            own = scores_of(k1[:end, :], queries)
            key_pos = lax.broadcasted_iota(jnp.int32, own.shape, 0)
            query_pos = at + lax.broadcasted_iota(jnp.int32, own.shape, 1)
            own = jnp.where(key_pos <= query_pos, own, -1e30)
            parts = [(own, v1[:, :end])]
            if with_earlier:
                parts.append((scores_of(k0[...], queries), v0[...]))
            out, log = attend(parts)
            o[:, at:end] = out.astype(jnp.bfloat16)
            l[0, :, at:end] = log

    @pl.when(flag_ref[0] % 2 == 1)
    def _():
        run(True)

    @pl.when(flag_ref[0] % 2 == 0)
    def _():
        run(False)


def merge_kernel(flag_ref, o, l, far_o, far_l, out):
    @pl.when(flag_ref[0] >= 2)
    def _():
        peak = jnp.maximum(l[0], far_l[0])
        here, there = jnp.exp2(l[0] - peak), jnp.exp2(far_l[0] - peak)
        mixed = (o[...].astype(jnp.float32) * here + far_o[...].astype(jnp.float32) * there) / (
            here + there
        )
        out[...] = jnp.transpose(mixed).astype(jnp.bfloat16)

    @pl.when(flag_ref[0] < 2)
    def _():
        out[...] = jnp.transpose(o[...].astype(jnp.float32)).astype(jnp.bfloat16)


def head_call(kernel, name, flag, rows, heads, ins, outs, work):
    specs = {
        "rows": (pl.BlockSpec((rows, HEAD), lambda h, f: (0, h)), (rows, heads * HEAD), jnp.bfloat16),
        "flat": (pl.BlockSpec((HEAD, rows), lambda h, f: (h, 0)), (heads * HEAD, rows), jnp.bfloat16),
        "log": (pl.BlockSpec((1, 1, rows), lambda h, f: (h, 0, 0)), (heads, 1, rows), jnp.float32),
    }
    return pl.pallas_call(
        kernel,
        grid_spec=pltpu.PrefetchScalarGridSpec(
            num_scalar_prefetch=1,
            grid=(heads,),
            in_specs=[specs[kind][0] for kind, _ in ins],
            out_specs=[specs[kind][0] for kind in outs],
        ),
        out_shape=[jax.ShapeDtypeStruct(specs[kind][1], specs[kind][2]) for kind in outs],
        compiler_params=params(24),
        cost_estimate=cost(
            4 * HEAD * work * heads, 2 * rows * HEAD * heads * len(ins), work * heads
        ),
        name=name,
    )(flag, *[x for _, x in ins])


def self_attention(normed, w_query, w_key, w_value, neighbours, w_cross_kv):
    rows = normed.shape[0]
    assert lax.axis_size("ctx") == 4
    ctx = lax.axis_index("ctx")
    width = w_query.shape[1] // 2
    heads = width // HEAD
    flag = ctx.reshape(1)
    merged = []
    for first in (0, width):
        q = project(normed, w_query, first, width)
        qa = lax.ppermute(q, "ctx", [(2, 1)])
        qb = lax.ppermute(q, "ctx", [(3, 1)])
        k = project(normed, w_key, first, width)
        k0 = lax.ppermute(k, "ctx", [(0, 1), (2, 3)])
        v = project(normed, w_value, first, width, flip=True)
        v0 = lax.ppermute(v, "ctx", [(0, 1), (2, 3)])
        if first == 0:
            qa, neighbours = lax.optimization_barrier((qa, neighbours))
            fetched = lax.all_gather(neighbours, "mp", axis=1, tiled=True)
        keys = [("rows", k0), ("flat", v0), ("rows", k), ("flat", v)]
        oa, la, ob, lb = head_call(
            far_kernel, "far_attention", flag, rows, heads,
            [("rows", qa), ("rows", qb)] + keys, ["flat", "log"] * 2, 4 * rows * rows,
        )
        far_a = [lax.ppermute(x, "ctx", [(1, 2)]) for x in (oa, la)]
        far_b = [lax.ppermute(x, "ctx", [(1, 3)]) for x in (ob, lb)]
        o, l = head_call(
            near_kernel, "near_attention", flag, rows, heads,
            [("rows", q)] + keys, ["flat", "log"], 2 * rows * rows,
        )
        if first == 0:
            kv, far_a = lax.optimization_barrier((neighbour_kv(fetched, w_cross_kv), far_a))
        far_o, far_l = [jnp.where(ctx == 3, b, a) for a, b in zip(far_a, far_b)]
        (out,) = head_call(
            merge_kernel, "merge", flag, rows, heads,
            [("flat", o), ("log", l), ("flat", far_o), ("log", far_l)], ["rows"], rows,
        )
        merged.append(out)
    return jnp.concatenate(merged, axis=1), kv


def fetch_neighbours(encoded, owners, slots):
    group_count = lax.axis_size(("pool", "ctx"))
    my_group = lax.axis_index(("pool", "ctx"))
    per_group = owners.size // group_count
    capacity = max(2, 2 * per_group // group_count)
    owner_table = owners.reshape(group_count, per_group)
    slot_table = slots.reshape(group_count, per_group)
    matched = (owner_table == my_group).astype(jnp.int32)
    order_rank = jnp.cumsum(matched, axis=1) - 1
    slot_index = jnp.arange(capacity, dtype=jnp.int32)
    picked = matched[:, None, :] * (order_rank[:, None, :] == slot_index[None, :, None]).astype(
        jnp.int32
    )
    source_rows = jnp.sum(picked * slot_table[:, None, :], axis=2).reshape(-1)
    outgoing = encoded[source_rows].reshape((group_count, capacity) + encoded.shape[1:])
    incoming = lax.all_to_all(outgoing, ("pool", "ctx"), split_axis=0, concat_axis=0, tiled=True)
    wanted = lax.dynamic_index_in_dim(owner_table, my_group, 0, keepdims=False)
    positions = jnp.arange(per_group, dtype=jnp.int32)
    same_owner = (wanted[:, None] == wanted[None, :]).astype(jnp.int32)
    before_this = (positions[None, :] < positions[:, None]).astype(jnp.int32)
    arrival = wanted * capacity + jnp.sum(same_owner * before_this, axis=1)
    arrived = incoming.reshape((group_count * capacity,) + encoded.shape[1:])[arrival]
    earlier = from_behind(arrived[-NB_PER:], "ctx", 1)
    extended = jnp.concatenate([earlier, arrived], axis=0)
    return extended


def neighbour_kernel(x_ref, w_ref, out_ref):
    out_ref[0] = jnp.dot(x_ref[...], w_ref[0], preferred_element_type=jnp.float32).astype(
        jnp.bfloat16
    )


def neighbour_kv(fetched, w_cross_kv):
    rows, depth = fetched.shape[0] * fetched.shape[1], fetched.shape[2]
    width = w_cross_kv.shape[2]
    tile = min(width, 256)
    steps = width // tile
    return pl.pallas_call(
        neighbour_kernel,
        grid=(2, steps),
        in_specs=[
            pl.BlockSpec((rows, depth), lambda c, j: (0, 0)),
            pl.BlockSpec((1, depth, tile), lambda c, j: (c, 0, j)),
        ],
        out_specs=pl.BlockSpec((1, rows, tile), lambda c, j: (c, 0, j)),
        out_shape=jax.ShapeDtypeStruct((2, rows, width), jnp.bfloat16),
        compiler_params=params(32, 2),
        cost_estimate=cost(4 * rows * depth * width, 4 * rows * width + 2 * rows * depth),
        name="neighbour_kv",
    )(in_hbm(fetched.reshape(rows, depth)), in_hbm(w_cross_kv))


def cross_kernel(q_ref, k_ref, v_ref, out_ref):
    rows = q_ref.shape[0]
    named = NB_PER * NB_TOK
    spans = rows // SPAN
    queries = pltpu.roll(q_ref[...].astype(jnp.float32), 1, 0).astype(jnp.bfloat16)

    parts = [queries[c * SPAN : (c + 1) * SPAN] for c in range(spans)] + [queries[:16]]
    scores = jnp.concatenate(
        [
            lax.dot_general(
                part,
                k_ref[0, c * named : (c + 1) * named, :],
                (((1,), (1,)), ((), ())),
                preferred_element_type=jnp.float32,
            )
            for c, part in enumerate(parts)
        ],
        axis=0,
    ) * (HEAD**-0.5 * LOG2E)
    weights = jnp.exp2(scores - jnp.max(scores, axis=1, keepdims=True))
    totals = jnp.sum(weights, axis=1, keepdims=True)
    weights = weights.astype(jnp.bfloat16)
    outs = [
        jnp.dot(
            weights[c * SPAN : c * SPAN + part.shape[0]],
            v_ref[0, c * named : (c + 1) * named, :],
            preferred_element_type=jnp.float32,
        )
        for c, part in enumerate(parts)
    ]
    whole = jnp.concatenate(outs, axis=0) / totals
    last, whole = whole[rows:], whole[:rows]
    last_row = jnp.broadcast_to(last[:1], whole.shape)
    row = lax.broadcasted_iota(jnp.int32, whole.shape, 0)
    whole = jnp.where(row == 0, last_row, whole)
    out_ref[...] = pltpu.roll(whole, rows - 1, 0).astype(jnp.bfloat16)


def cross_attention(queries, kv):
    rows, width = queries.shape
    heads = width // HEAD
    return pl.pallas_call(
        cross_kernel,
        grid=(heads,),
        in_specs=[
            pl.BlockSpec((rows, HEAD), lambda h: (0, h)),
            pl.BlockSpec((1, kv.shape[1], HEAD), lambda h: (0, 0, h)),
            pl.BlockSpec((1, kv.shape[1], HEAD), lambda h: (1, 0, h)),
        ],
        out_specs=pl.BlockSpec((rows, HEAD), lambda h: (0, h)),
        out_shape=jax.ShapeDtypeStruct((rows, width), jnp.bfloat16),
        compiler_params=params(24),
        cost_estimate=cost(1024 * rows * width, 4 * kv.shape[1] * width, 2 * rows * width),
        name="cross_attention",
    )(queries, kv, kv)


def per_device(
    tokens,
    norm_gain,
    cross_gain,
    w_query,
    w_key,
    w_value,
    w_out,
    w_cross_query,
    w_cross_kv,
    w_cross_out,
    encoded,
    owners,
    slots,
):
    own = tokens[0]
    normed = normalised(gather_blocks(own), norm_gain)
    neighbours = fetch_neighbours(encoded, owners, slots)
    attended, kv = self_attention(normed, w_query, w_key, w_value, neighbours, w_cross_kv)
    share = project_scattered(attended, w_out)
    residual = (own.astype(jnp.float32) + share).astype(jnp.bfloat16)
    cross_in = normalised(gather_blocks(residual), cross_gain)
    cross_queries = project(cross_in, w_cross_query, 0, w_cross_query.shape[1])
    crossed = cross_attention(cross_queries, kv)
    cross_part = project_scattered(crossed, w_cross_out)
    return (residual.astype(jnp.float32) + cross_part).astype(jnp.bfloat16)[None]


def solution(mesh):
    placed = (
        P("pool", "ctx", "mp"),
        P(),
        P(),
        P(None, "mp"),
        P(None, "mp"),
        P(None, "mp"),
        P("mp", None),
        P(None, "mp"),
        P(None, None, "mp"),
        P("mp", None),
        P(("pool", "ctx"), "mp", None),
        P(),
        P(),
    )
    return jax.shard_map(
        per_device, mesh=mesh, in_specs=placed, out_specs=P("pool", "ctx", "mp"), check_vma=False
    )
```

```python
import functools

import jax
import jax.numpy as jnp
from jax import lax
from jax.experimental import pallas as pl
from jax.experimental.pallas import tpu as pltpu
from jax.sharding import PartitionSpec as P

HEAD = 128
SPAN = 64
NB_TOK = 128
NB_PER = 2
MIB = 1 << 20
LOG2E = 1.4426950408889634

norm_eps = 1e-05


def params(mib, steps=1):
    return pltpu.CompilerParams(
        vmem_limit_bytes=mib * MIB, dimension_semantics=("arbitrary",) * steps
    )


def cost(flops, moved, exps=0):
    return pl.CostEstimate(flops=int(flops), bytes_accessed=int(moved), transcendentals=int(exps))


def in_hbm(weight):
    return pltpu.with_memory_space_constraint(weight, pltpu.HBM)


def swap(block, bit):
    return lax.ppermute(block, "mp", [(i, i ^ bit) for i in range(lax.axis_size("mp"))])


def gather_blocks(block):
    count = lax.axis_size("mp")
    blocks = {0: block}
    bit = count // 2
    while bit:
        blocks.update({o ^ bit: swap(b, bit) for o, b in list(blocks.items())})
        bit //= 2
    return [blocks[o] for o in range(count)]


def scatter_sum(partials):
    count = lax.axis_size("mp")
    held = dict(enumerate(partials))
    bit = 1
    while bit < count:
        summed = {}
        for o in sorted((o for o in held if not o & bit), reverse=True):
            total = held[o].astype(jnp.float32) + swap(held[o | bit], bit).astype(jnp.float32)
            summed[o] = total if 2 * bit == count else total.astype(jnp.bfloat16)
        held = summed
        bit *= 2
    return held[0]


def norm_kernel(place_ref, gain_ref, *refs):
    *blocks, out_ref = refs
    width = blocks[0].shape[1]
    features = width * len(blocks)
    squares = 0.0
    for b in blocks:
        x = b[...].astype(jnp.float32)
        squares += jnp.sum(x * x, axis=1, keepdims=True)
    scale = lax.rsqrt(squares / features + norm_eps)
    for o, b in enumerate(blocks):
        columns = pl.ds(pl.multiple_of(place_ref[o] * width, width), width)
        out_ref[:, columns] = (b[...].astype(jnp.float32) * scale * gain_ref[:, columns]).astype(
            jnp.bfloat16
        )


def normalised(blocks, gain):
    rows, width = blocks[0].shape
    features = width * len(blocks)
    tile = min(rows, 128)
    places = lax.axis_index("mp") ^ jnp.arange(len(blocks), dtype=jnp.int32)
    return pl.pallas_call(
        norm_kernel,
        grid_spec=pltpu.PrefetchScalarGridSpec(
            num_scalar_prefetch=1,
            grid=(rows // tile,),
            in_specs=[pl.BlockSpec((1, features), lambda i, p: (0, 0))]
            + [pl.BlockSpec((tile, width), lambda i, p: (i, 0))] * len(blocks),
            out_specs=pl.BlockSpec((tile, features), lambda i, p: (i, 0)),
        ),
        out_shape=jax.ShapeDtypeStruct((rows, features), jnp.bfloat16),
        compiler_params=params(24),
        cost_estimate=cost(6 * rows * features, 4 * rows * features),
        name="norm",
    )(places, gain.reshape(1, features), *blocks)


def project_kernel(x_ref, w_ref, out_ref):
    out_ref[...] = jnp.dot(x_ref[...], w_ref[...], preferred_element_type=jnp.float32).astype(
        jnp.bfloat16
    )


def project(x, w, first, width):
    rows, depth = x.shape
    tile = min(width, 256)
    base = first // tile
    return pl.pallas_call(
        project_kernel,
        grid=(width // tile,),
        in_specs=[
            pl.BlockSpec((rows, depth), lambda j: (0, 0)),
            pl.BlockSpec((depth, tile), lambda j: (0, base + j)),
        ],
        out_specs=pl.BlockSpec((rows, tile), lambda j: (0, j)),
        out_shape=jax.ShapeDtypeStruct((rows, width), jnp.bfloat16),
        compiler_params=params(24),
        cost_estimate=cost(2 * rows * depth * width, 2 * depth * (rows + width)),
        name="project",
    )(x, in_hbm(w))


def pair_kernel(steps, x_ref, wk_ref, wv_ref, out_ref):
    def write(w_ref):
        out_ref[...] = jnp.dot(
            x_ref[...], w_ref[...], preferred_element_type=jnp.float32
        ).astype(jnp.bfloat16)

    @pl.when(pl.program_id(0) < steps)
    def _():
        write(wk_ref)

    @pl.when(pl.program_id(0) >= steps)
    def _():
        write(wv_ref)


def project_pair(x, w_key, w_value, first, width):
    rows, depth = x.shape
    tile = min(width, 256)
    base, steps = first // tile, width // tile
    return pl.pallas_call(
        functools.partial(pair_kernel, steps),
        grid=(2 * steps,),
        in_specs=[
            pl.BlockSpec((rows, depth), lambda j: (0, 0)),
            pl.BlockSpec((depth, tile), lambda j: (0, base + jnp.minimum(j, steps - 1))),
            pl.BlockSpec((depth, tile), lambda j: (0, base + jnp.maximum(j - steps, 0))),
        ],
        out_specs=pl.BlockSpec((rows, tile), lambda j: (0, j)),
        out_shape=jax.ShapeDtypeStruct((rows, 2 * width), jnp.bfloat16),
        compiler_params=params(28),
        cost_estimate=cost(4 * rows * depth * width, 2 * depth * (rows + 2 * width)),
        name="project_pair",
    )(x, in_hbm(w_key), in_hbm(w_value))


def block_kernel(place_ref, x_ref, w_ref, out_ref):
    out_ref[...] = jnp.dot(
        x_ref[...], w_ref[...], preferred_element_type=jnp.float32
    ).astype(jnp.bfloat16)


def project_block(x, w, place, width):
    rows, depth = x.shape
    tile = min(width, 512)
    steps = width // tile
    return pl.pallas_call(
        block_kernel,
        grid_spec=pltpu.PrefetchScalarGridSpec(
            num_scalar_prefetch=1,
            grid=(steps,),
            in_specs=[
                pl.BlockSpec((rows, depth), lambda j, p: (0, 0)),
                pl.BlockSpec((depth, tile), lambda j, p: (0, p[0] * steps + j)),
            ],
            out_specs=pl.BlockSpec((rows, tile), lambda j, p: (0, j)),
        ),
        out_shape=jax.ShapeDtypeStruct((rows, width), jnp.bfloat16),
        compiler_params=params(16),
        cost_estimate=cost(2 * rows * depth * width, 2 * depth * (rows + width)),
        name="project_block",
    )(place.reshape(1), x, in_hbm(w))


def project_scattered(x, w):
    count = lax.axis_size("mp")
    width = w.shape[1] // count
    me = lax.axis_index("mp")
    partials = {}
    for o in sorted(range(count), key=lambda o: (1 - o % 2, -o)):
        partials[o] = project_block(x, w, me ^ o, width)
    return scatter_sum([partials[o] for o in range(count)])


def scores_of(keys, queries):
    return lax.dot_general(
        keys, queries, (((1,), (1,)), ((), ())), preferred_element_type=jnp.float32
    ) * (HEAD**-0.5 * LOG2E)


def attend(parts):
    peak = functools.reduce(jnp.maximum, [jnp.max(s, axis=0, keepdims=True) for s, _ in parts])
    total, out = 0.0, 0.0
    for s, values in parts:
        weights = jnp.exp2(s - peak)
        total += jnp.sum(weights, axis=0, keepdims=True)
        out += jnp.dot(values, weights.astype(jnp.bfloat16), preferred_element_type=jnp.float32)
    return out / total, peak + jnp.log2(total)


def turned(values):
    return jnp.transpose(values[...].astype(jnp.float32)).astype(jnp.bfloat16)


def far_kernel(flag_ref, qa, qb, k0, v0, k1, v1, oa, la, ob, lb):
    rows = qa.shape[0]
    tile = min(rows, 256)

    @pl.when(flag_ref[0] == 1)
    def _():
        flat0, flat1 = turned(v0), turned(v1)
        for q, o, l in ((qa, oa, la), (qb, ob, lb)):
            for at in range(0, rows, tile):
                queries = q[at : at + tile, :]
                out, log = attend(
                    [(scores_of(k0[...], queries), flat0), (scores_of(k1[...], queries), flat1)]
                )
                o[:, at : at + tile] = out.astype(jnp.bfloat16)
                l[0, :, at : at + tile] = log


def near_kernel(flag_ref, q, k0, v0, k1, v1, o, l):
    rows = q.shape[0]
    tile = min(rows, 256)

    def run(with_earlier):
        flat1 = turned(v1)
        flat0 = turned(v0) if with_earlier else None
        for at in range(0, rows, tile):
            queries = q[at : at + tile, :]
            end = at + tile
            own = scores_of(k1[:end, :], queries)
            key_pos = lax.broadcasted_iota(jnp.int32, own.shape, 0)
            query_pos = at + lax.broadcasted_iota(jnp.int32, own.shape, 1)
            own = jnp.where(key_pos <= query_pos, own, -1e30)
            parts = [(own, flat1[:, :end])]
            if with_earlier:
                parts.append((scores_of(k0[...], queries), flat0))
            out, log = attend(parts)
            o[:, at:end] = out.astype(jnp.bfloat16)
            l[0, :, at:end] = log

    @pl.when(flag_ref[0] % 2 == 1)
    def _():
        run(True)

    @pl.when(flag_ref[0] % 2 == 0)
    def _():
        run(False)


def merge_kernel(flag_ref, o, l, far_o, far_l, out):
    @pl.when(flag_ref[0] >= 2)
    def _():
        peak = jnp.maximum(l[0], far_l[0])
        here, there = jnp.exp2(l[0] - peak), jnp.exp2(far_l[0] - peak)
        mixed = (o[...].astype(jnp.float32) * here + far_o[...].astype(jnp.float32) * there) / (
            here + there
        )
        out[...] = jnp.transpose(mixed).astype(jnp.bfloat16)

    @pl.when(flag_ref[0] < 2)
    def _():
        out[...] = jnp.transpose(o[...].astype(jnp.float32)).astype(jnp.bfloat16)


def head_call(kernel, name, flag, rows, heads, ins, outs, work):
    specs = {
        "rows": (pl.BlockSpec((rows, HEAD), lambda h, f: (0, h)), (rows, heads * HEAD), jnp.bfloat16),
        "values": (pl.BlockSpec((rows, HEAD), lambda h, f: (0, heads + h)), None, None),
        "flat": (pl.BlockSpec((HEAD, rows), lambda h, f: (h, 0)), (heads * HEAD, rows), jnp.bfloat16),
        "log": (pl.BlockSpec((1, 1, rows), lambda h, f: (h, 0, 0)), (heads, 1, rows), jnp.float32),
    }
    call = pl.pallas_call(
        kernel,
        grid_spec=pltpu.PrefetchScalarGridSpec(
            num_scalar_prefetch=1,
            grid=(heads,),
            in_specs=[specs[kind][0] for kind, _ in ins],
            out_specs=[specs[kind][0] for kind in outs],
        ),
        out_shape=[jax.ShapeDtypeStruct(specs[kind][1], specs[kind][2]) for kind in outs],
        compiler_params=params(24),
        cost_estimate=cost(
            4 * HEAD * work * heads, 2 * rows * HEAD * heads * len(ins), work * heads
        ),
        name=name,
    )
    return list(call(flag, *[x for _, x in ins]))


def self_attention(normed, w_query, w_key, w_value, neighbours, w_cross_kv):
    rows = normed.shape[0]
    assert lax.axis_size("ctx") == 4
    ctx = lax.axis_index("ctx")
    width = w_query.shape[1] // 2
    heads = width // HEAD
    flag = ctx.reshape(1)
    q = project(normed, w_query, 0, 2 * width)
    qa = lax.ppermute(q, "ctx", [(2, 1)])
    qb = lax.ppermute(q, "ctx", [(3, 1)])
    normed, q = lax.optimization_barrier((normed, q))
    halves = []
    for first in (0, width):
        pair = project_pair(normed, w_key, w_value, first, width)
        pair0 = lax.ppermute(pair, "ctx", [(0, 1), (2, 3)])
        normed, pair = lax.optimization_barrier((normed, pair))
        halves.append([pair, pair0])
    incoming, arrival, wanted = neighbours
    incoming, halves[1][0] = lax.optimization_barrier((incoming, halves[1][0]))
    arrived = jnp.where((wanted >= 0)[:, None, None], incoming[arrival], jnp.zeros((), incoming.dtype))
    fetched = lax.all_gather(arrived, "mp", axis=1, tiled=True)
    arrived, qa = lax.optimization_barrier((arrived, qa))
    fars = []
    for part, (pair, pair0) in zip(("rows", "values"), halves):
        if fars:
            qa, fars[0][0] = lax.optimization_barrier((qa, fars[0][0]))
        keys = [("rows", pair0), ("values", pair0), ("rows", pair), ("values", pair)]
        fars.append(
            head_call(
                far_kernel, "far_attention", flag, rows, heads,
                [(part, qa), (part, qb)] + keys, ["flat", "log"] * 2, 4 * rows * rows,
            )
        )
    fars[1][0], q = lax.optimization_barrier((fars[1][0], q))
    sent = [
        [lax.ppermute(x, "ctx", [(1, 2 + at // 2)]) for at, x in enumerate(far)] for far in fars
    ]
    nears = []
    for part, (pair, pair0) in zip(("rows", "values"), halves):
        keys = [("rows", pair0), ("values", pair0), ("rows", pair), ("values", pair)]
        nears.append(
            head_call(
                near_kernel, "near_attention", flag, rows, heads,
                [(part, q)] + keys, ["flat", "log"], 2 * rows * rows,
            )
        )
    fetched, nears = lax.optimization_barrier((fetched, nears))
    kv, nears = lax.optimization_barrier((neighbour_kv(fetched, w_cross_kv), nears))
    merged = []
    for (o, l), (oa, la, ob, lb) in zip(nears, sent):
        far_o, far_l = jnp.where(ctx == 3, ob, oa), jnp.where(ctx == 3, lb, la)
        (out,) = head_call(
            merge_kernel, "merge", flag, rows, heads,
            [("flat", o), ("log", l), ("flat", far_o), ("log", far_l)], ["rows"], rows,
        )
        merged.append(out)
    return jnp.concatenate(merged, axis=1), kv


def fetch_neighbours(encoded, owners, slots):
    group_count = lax.axis_size(("pool", "ctx"))
    my_group = lax.axis_index(("pool", "ctx"))
    per_group = owners.size // group_count
    capacity = max(2, 2 * per_group // group_count) + 1

    def with_earlier(table, missing):
        grouped = table.reshape(-1, lax.axis_size("ctx"), per_group)
        earlier = jnp.pad(
            grouped[:, :-1, -NB_PER:], ((0, 0), (1, 0), (0, 0)), constant_values=missing
        )
        return jnp.concatenate([earlier, grouped], axis=2).reshape(group_count, -1)

    owner_table = with_earlier(owners, -1)
    slot_table = with_earlier(slots, 0)
    matched = (owner_table == my_group).astype(jnp.int32)
    order_rank = jnp.cumsum(matched, axis=1) - 1
    slot_index = jnp.arange(capacity, dtype=jnp.int32)
    picked = matched[:, None, :] * (order_rank[:, None, :] == slot_index[None, :, None]).astype(
        jnp.int32
    )
    source_rows = jnp.sum(picked * slot_table[:, None, :], axis=2).reshape(-1)
    outgoing = encoded[source_rows].reshape((group_count, capacity) + encoded.shape[1:])
    incoming = lax.all_to_all(outgoing, ("pool", "ctx"), split_axis=0, concat_axis=0, tiled=True)
    wanted = lax.dynamic_index_in_dim(owner_table, my_group, 0, keepdims=False)
    positions = jnp.arange(wanted.shape[0], dtype=jnp.int32)
    same_owner = (wanted[:, None] == wanted[None, :]).astype(jnp.int32)
    before_this = (positions[None, :] < positions[:, None]).astype(jnp.int32)
    arrival = jnp.maximum(wanted, 0) * capacity + jnp.sum(same_owner * before_this, axis=1)
    return incoming.reshape((group_count * capacity,) + encoded.shape[1:]), arrival, wanted


def neighbour_kernel(x_ref, w_ref, out_ref):
    out_ref[0] = jnp.dot(x_ref[...], w_ref[0], preferred_element_type=jnp.float32).astype(
        jnp.bfloat16
    )


def neighbour_kv(fetched, w_cross_kv):
    rows, depth = fetched.shape[0] * fetched.shape[1], fetched.shape[2]
    width = w_cross_kv.shape[2]
    tile = min(width, 256)
    steps = width // tile
    return pl.pallas_call(
        neighbour_kernel,
        grid=(2, steps),
        in_specs=[
            pl.BlockSpec((rows, depth), lambda c, j: (0, 0)),
            pl.BlockSpec((1, depth, tile), lambda c, j: (c, 0, j)),
        ],
        out_specs=pl.BlockSpec((1, rows, tile), lambda c, j: (c, 0, j)),
        out_shape=jax.ShapeDtypeStruct((2, rows, width), jnp.bfloat16),
        compiler_params=params(32, 2),
        cost_estimate=cost(4 * rows * depth * width, 4 * rows * width + 2 * rows * depth),
        name="neighbour_kv",
    )(in_hbm(fetched.reshape(rows, depth)), in_hbm(w_cross_kv))


def cross_kernel(q_ref, k_ref, v_ref, out_ref):
    rows = q_ref.shape[0]
    named = NB_PER * NB_TOK
    spans = rows // SPAN
    queries = pltpu.roll(q_ref[...].astype(jnp.float32), 1, 0).astype(jnp.bfloat16)

    parts = [queries[c * SPAN : (c + 1) * SPAN] for c in range(spans)] + [queries[:16]]
    scores = jnp.concatenate(
        [
            lax.dot_general(
                part,
                k_ref[0, c * named : (c + 1) * named, :],
                (((1,), (1,)), ((), ())),
                preferred_element_type=jnp.float32,
            )
            for c, part in enumerate(parts)
        ],
        axis=0,
    ) * (HEAD**-0.5 * LOG2E)
    weights = jnp.exp2(scores - jnp.max(scores, axis=1, keepdims=True))
    totals = jnp.sum(weights, axis=1, keepdims=True)
    weights = weights.astype(jnp.bfloat16)
    outs = [
        jnp.dot(
            weights[c * SPAN : c * SPAN + part.shape[0]],
            v_ref[0, c * named : (c + 1) * named, :],
            preferred_element_type=jnp.float32,
        )
        for c, part in enumerate(parts)
    ]
    whole = jnp.concatenate(outs, axis=0) / totals
    last, whole = whole[rows:], whole[:rows]
    last_row = jnp.broadcast_to(last[:1], whole.shape)
    row = lax.broadcasted_iota(jnp.int32, whole.shape, 0)
    whole = jnp.where(row == 0, last_row, whole)
    out_ref[...] = pltpu.roll(whole, rows - 1, 0).astype(jnp.bfloat16)


def cross_attention(queries, kv):
    rows, width = queries.shape
    heads = width // HEAD
    return pl.pallas_call(
        cross_kernel,
        grid=(heads,),
        in_specs=[
            pl.BlockSpec((rows, HEAD), lambda h: (0, h)),
            pl.BlockSpec((1, kv.shape[1], HEAD), lambda h: (0, 0, h)),
            pl.BlockSpec((1, kv.shape[1], HEAD), lambda h: (1, 0, h)),
        ],
        out_specs=pl.BlockSpec((rows, HEAD), lambda h: (0, h)),
        out_shape=jax.ShapeDtypeStruct((rows, width), jnp.bfloat16),
        compiler_params=params(24),
        cost_estimate=cost(1024 * rows * width, 4 * kv.shape[1] * width, 2 * rows * width),
        name="cross_attention",
    )(queries, kv, kv)


def per_device(
    tokens,
    norm_gain,
    cross_gain,
    w_query,
    w_key,
    w_value,
    w_out,
    w_cross_query,
    w_cross_kv,
    w_cross_out,
    encoded,
    owners,
    slots,
):
    own = tokens[0]
    blocks = gather_blocks(own)
    blocks[1], owners, slots = lax.optimization_barrier((blocks[1], owners, slots))
    normed = normalised(blocks, norm_gain)
    neighbours = fetch_neighbours(encoded, owners, slots)
    attended, kv = self_attention(normed, w_query, w_key, w_value, neighbours, w_cross_kv)
    share = project_scattered(attended, w_out)
    residual = (own.astype(jnp.float32) + share).astype(jnp.bfloat16)
    cross_in = normalised(gather_blocks(residual), cross_gain)
    cross_queries = project(cross_in, w_cross_query, 0, w_cross_query.shape[1])
    crossed = cross_attention(cross_queries, kv)
    cross_part = project_scattered(crossed, w_cross_out)
    return (residual.astype(jnp.float32) + cross_part).astype(jnp.bfloat16)[None]


def solution(mesh):
    placed = (
        P("pool", "ctx", "mp"),
        P(),
        P(),
        P(None, "mp"),
        P(None, "mp"),
        P(None, "mp"),
        P("mp", None),
        P(None, "mp"),
        P(None, None, "mp"),
        P("mp", None),
        P(("pool", "ctx"), "mp", None),
        P(),
        P(),
    )
    return jax.shard_map(
        per_device, mesh=mesh, in_specs=placed, out_specs=P("pool", "ctx", "mp"), check_vma=False
    )
```

```python
import functools

import jax
import jax.numpy as jnp
from jax import lax
from jax.experimental import pallas as pl
from jax.experimental.pallas import tpu as pltpu
from jax.sharding import PartitionSpec as P

HEAD = 128
SPAN = 64
NB_TOK = 128
NB_PER = 2
MIB = 1 << 20
LOG2E = 1.4426950408889634
EXTRA = 16

norm_eps = 1e-05


def params(mib, steps=1):
    return pltpu.CompilerParams(
        vmem_limit_bytes=mib * MIB, dimension_semantics=("arbitrary",) * steps
    )


def cost(flops, moved, exps=0):
    return pl.CostEstimate(flops=int(flops), bytes_accessed=int(moved), transcendentals=int(exps))


def in_hbm(weight):
    return pltpu.with_memory_space_constraint(weight, pltpu.HBM)


def swap(block, bit):
    return lax.ppermute(block, "mp", [(i, i ^ bit) for i in range(lax.axis_size("mp"))])


def gather_blocks(block):
    count = lax.axis_size("mp")
    blocks = {0: block}
    bit = count // 2
    while bit:
        blocks.update({o ^ bit: swap(b, bit) for o, b in list(blocks.items())})
        bit //= 2
    return [blocks[o] for o in range(count)]


def scatter_sum(partials):
    count = lax.axis_size("mp")
    held = dict(enumerate(partials))
    bit = 1
    while bit < count:
        summed = {}
        for o in sorted((o for o in held if not o & bit), reverse=True):
            total = held[o].astype(jnp.float32) + swap(held[o | bit], bit).astype(jnp.float32)
            summed[o] = total if 2 * bit == count else total.astype(jnp.bfloat16)
        held = summed
        bit *= 2
    return held[0]


def norm_kernel(place_ref, gain_ref, *refs):
    *blocks, out_ref = refs
    width = blocks[0].shape[1]
    features = width * len(blocks)
    squares = 0.0
    for b in blocks:
        x = b[...].astype(jnp.float32)
        squares += jnp.sum(x * x, axis=1, keepdims=True)
    scale = lax.rsqrt(squares / features + norm_eps)
    for o, b in enumerate(blocks):
        columns = pl.ds(pl.multiple_of(place_ref[o] * width, width), width)
        out_ref[:, columns] = (b[...].astype(jnp.float32) * scale * gain_ref[:, columns]).astype(
            jnp.bfloat16
        )


def normalised(blocks, gain):
    rows, width = blocks[0].shape
    features = width * len(blocks)
    tile = min(rows, 128)
    places = lax.axis_index("mp") ^ jnp.arange(len(blocks), dtype=jnp.int32)
    return pl.pallas_call(
        norm_kernel,
        grid_spec=pltpu.PrefetchScalarGridSpec(
            num_scalar_prefetch=1,
            grid=(rows // tile,),
            in_specs=[pl.BlockSpec((1, features), lambda i, p: (0, 0))]
            + [pl.BlockSpec((tile, width), lambda i, p: (i, 0))] * len(blocks),
            out_specs=pl.BlockSpec((tile, features), lambda i, p: (i, 0)),
        ),
        out_shape=jax.ShapeDtypeStruct((rows, features), jnp.bfloat16),
        compiler_params=params(24),
        cost_estimate=cost(6 * rows * features, 4 * rows * features),
        name="norm",
    )(places, gain.reshape(1, features), *blocks)


def project_kernel(flip, x_ref, w_ref, out_ref):
    product = jnp.dot(x_ref[...], w_ref[...], preferred_element_type=jnp.float32)
    if flip:
        product = jnp.transpose(product)
    out_ref[...] = product.astype(jnp.bfloat16)


def project(x, w, first, width, flip=False):
    rows, depth = x.shape
    tile = min(width, 256)
    base = first // tile
    if flip:
        out_spec, out_dims = pl.BlockSpec((tile, rows), lambda j: (j, 0)), (width, rows)
    else:
        out_spec, out_dims = pl.BlockSpec((rows, tile), lambda j: (0, j)), (rows, width)
    return pl.pallas_call(
        functools.partial(project_kernel, flip),
        grid=(width // tile,),
        in_specs=[
            pl.BlockSpec((rows, depth), lambda j: (0, 0)),
            pl.BlockSpec((depth, tile), lambda j: (0, base + j)),
        ],
        out_specs=out_spec,
        out_shape=jax.ShapeDtypeStruct(out_dims, jnp.bfloat16),
        compiler_params=params(24),
        cost_estimate=cost(2 * rows * depth * width, 2 * depth * (rows + width)),
        name="project",
    )(x, in_hbm(w))


def block_kernel(place_ref, x_ref, w_ref, out_ref):
    out_ref[...] = jnp.dot(
        x_ref[...], w_ref[...], preferred_element_type=jnp.float32
    ).astype(jnp.bfloat16)


def project_block(x, w, place, width):
    rows, depth = x.shape
    tile = min(width, 512)
    steps = width // tile
    return pl.pallas_call(
        block_kernel,
        grid_spec=pltpu.PrefetchScalarGridSpec(
            num_scalar_prefetch=1,
            grid=(steps,),
            in_specs=[
                pl.BlockSpec((rows, depth), lambda j, p: (0, 0)),
                pl.BlockSpec((depth, tile), lambda j, p: (0, p[0] * steps + j)),
            ],
            out_specs=pl.BlockSpec((rows, tile), lambda j, p: (0, j)),
        ),
        out_shape=jax.ShapeDtypeStruct((rows, width), jnp.bfloat16),
        compiler_params=params(16),
        cost_estimate=cost(2 * rows * depth * width, 2 * depth * (rows + width)),
        name="project_block",
    )(place.reshape(1), x, in_hbm(w))


def project_scattered(x, w):
    count = lax.axis_size("mp")
    width = w.shape[1] // count
    me = lax.axis_index("mp")
    partials = {}
    for o in reversed(range(count)):
        partials[o] = project_block(x, w, me ^ o, width)
        partials[o], x = lax.optimization_barrier((partials[o], x))
    return scatter_sum([partials[o] for o in range(count)])


def scores_of(keys, queries):
    return lax.dot_general(
        keys, queries, (((1,), (1,)), ((), ())), preferred_element_type=jnp.float32
    ) * (HEAD**-0.5 * LOG2E)


def attend(parts):
    peak = functools.reduce(jnp.maximum, [jnp.max(s, axis=0, keepdims=True) for s, _ in parts])
    total, out = 0.0, 0.0
    for s, values in parts:
        weights = jnp.exp2(s - peak)
        total += jnp.sum(weights, axis=0, keepdims=True)
        out += jnp.dot(values, weights.astype(jnp.bfloat16), preferred_element_type=jnp.float32)
    return out / total, peak + jnp.log2(total)


def far_kernel(flag_ref, qa, qb, k0, v0, k1, v1, oa, ob):
    rows = qa.shape[0]
    tile = min(rows, 256)

    @pl.when(flag_ref[0] == 1)
    def _():
        for q, o in ((qa, oa), (qb, ob)):
            for at in range(0, rows, tile):
                queries = q[at : at + tile, :]
                out, log = attend(
                    [(scores_of(k0[...], queries), v0[...]), (scores_of(k1[...], queries), v1[...])]
                )
                o[:HEAD, at : at + tile] = out.astype(jnp.bfloat16)
                high = log.astype(jnp.bfloat16).astype(jnp.float32)
                middle = (log - high).astype(jnp.bfloat16).astype(jnp.float32)
                row = lax.broadcasted_iota(jnp.int32, (EXTRA, tile), 0)
                pieces = jnp.where(
                    row == 0,
                    high,
                    jnp.where(row == 1, middle, jnp.where(row == 2, log - high - middle, 0.0)),
                )
                o[HEAD:, at : at + tile] = pieces.astype(jnp.bfloat16)


def near_kernel(flag_ref, q, k0, v0, k1, v1, o, l):
    rows = q.shape[0]
    tile = min(rows, 256)

    def run(with_earlier):
        for at in range(0, rows, tile):
            queries = q[at : at + tile, :]
            end = at + tile
            own = scores_of(k1[:end, :], queries)
            key_pos = lax.broadcasted_iota(jnp.int32, own.shape, 0)
            query_pos = at + lax.broadcasted_iota(jnp.int32, own.shape, 1)
            own = jnp.where(key_pos <= query_pos, own, -1e30)
            parts = [(own, v1[:, :end])]
            if with_earlier:
                parts.append((scores_of(k0[...], queries), v0[...]))
            out, log = attend(parts)
            o[:, at:end] = out.astype(jnp.bfloat16)
            l[0, :, at:end] = log

    @pl.when(flag_ref[0] % 2 == 1)
    def _():
        run(True)

    @pl.when(flag_ref[0] % 2 == 0)
    def _():
        run(False)


def merge_kernel(flag_ref, o, l, far_o, out):
    @pl.when(flag_ref[0] >= 2)
    def _():
        pieces = far_o[HEAD:, :].astype(jnp.float32)
        far_l = pieces[0:1] + pieces[1:2] + pieces[2:3]
        peak = jnp.maximum(l[0], far_l)
        here, there = jnp.exp2(l[0] - peak), jnp.exp2(far_l - peak)
        mixed = (o[...].astype(jnp.float32) * here + far_o[:HEAD, :].astype(jnp.float32) * there) / (
            here + there
        )
        out[...] = jnp.transpose(mixed).astype(jnp.bfloat16)

    @pl.when(flag_ref[0] < 2)
    def _():
        out[...] = jnp.transpose(o[...].astype(jnp.float32)).astype(jnp.bfloat16)


def head_call(kernel, name, flag, rows, heads, ins, outs, work):
    specs = {
        "rows": (pl.BlockSpec((rows, HEAD), lambda h, f: (0, h)), (rows, heads * HEAD), jnp.bfloat16),
        "flat": (pl.BlockSpec((HEAD, rows), lambda h, f: (h, 0)), (heads * HEAD, rows), jnp.bfloat16),
        "sent": (
            pl.BlockSpec((HEAD + EXTRA, rows), lambda h, f: (h, 0)),
            (heads * (HEAD + EXTRA), rows),
            jnp.bfloat16,
        ),
        "log": (pl.BlockSpec((1, 1, rows), lambda h, f: (h, 0, 0)), (heads, 1, rows), jnp.float32),
    }
    call = pl.pallas_call(
        kernel,
        grid_spec=pltpu.PrefetchScalarGridSpec(
            num_scalar_prefetch=1,
            grid=(heads,),
            in_specs=[specs[kind][0] for kind, _ in ins],
            out_specs=[specs[kind][0] for kind in outs],
        ),
        out_shape=[jax.ShapeDtypeStruct(specs[kind][1], specs[kind][2]) for kind in outs],
        compiler_params=params(24),
        cost_estimate=cost(
            4 * HEAD * work * heads, 2 * rows * HEAD * heads * len(ins), work * heads
        ),
        name=name,
    )
    return list(call(flag, *[x for _, x in ins]))


def self_attention(normed, w_query, w_key, w_value, neighbours, w_cross_kv):
    rows = normed.shape[0]
    assert lax.axis_size("ctx") == 4
    ctx = lax.axis_index("ctx")
    width = w_query.shape[1] // 2
    heads = width // HEAD
    flag = ctx.reshape(1)
    halves, fars = [], []
    for first in (0, width):
        q = project(normed, w_query, first, width)
        qa = lax.ppermute(q, "ctx", [(2, 1)])
        qb = lax.ppermute(q, "ctx", [(3, 1)])
        k = project(normed, w_key, first, width)
        k0 = lax.ppermute(k, "ctx", [(0, 1), (2, 3)])
        v = project(normed, w_value, first, width, flip=True)
        v0 = lax.ppermute(v, "ctx", [(0, 1), (2, 3)])
        normed, v = lax.optimization_barrier((normed, v))
        halves.append([q, qa, qb, k, k0, v, v0])
    incoming, arrival, wanted = neighbours
    incoming, halves[0][5] = lax.optimization_barrier((incoming, halves[0][5]))
    arrived = jnp.where((wanted >= 0)[:, None, None], incoming[arrival], jnp.zeros((), incoming.dtype))
    fetched = lax.all_gather(arrived, "mp", axis=1, tiled=True)
    arrived, halves[0][1] = lax.optimization_barrier((arrived, halves[0][1]))
    for at, (q, qa, qb, k, k0, v, v0) in enumerate(halves):
        keys = [("rows", k0), ("flat", v0), ("rows", k), ("flat", v)]
        far = head_call(
            far_kernel, "far_attention", flag, rows, heads,
            [("rows", qa), ("rows", qb)] + keys, ["sent"] * 2, 4 * rows * rows,
        )
        halves[at] = (q, keys)
        fars.append(far)
    last, fetched = lax.optimization_barrier((fars[1][1], fetched))
    kv, queries = lax.optimization_barrier(
        (neighbour_kv(fetched, w_cross_kv), [q for q, _ in halves])
    )
    fars[1][1] = last
    sent = [
        [lax.ppermute(x, "ctx", [(1, 2 + at)]) for at, x in enumerate(far)] for far in fars
    ]
    nears = [
        head_call(
            near_kernel, "near_attention", flag, rows, heads,
            [("rows", q)] + keys, ["flat", "log"], 2 * rows * rows,
        )
        for q, (_, keys) in zip(queries, halves)
    ]
    merged = []
    for (o, l), (oa, ob) in zip(nears, sent):
        far_o = jnp.where(ctx == 3, ob, oa)
        (out,) = head_call(
            merge_kernel, "merge", flag, rows, heads,
            [("flat", o), ("log", l), ("sent", far_o)], ["rows"], rows,
        )
        merged.append(out)
    return jnp.concatenate(merged, axis=1), kv


def fetch_neighbours(encoded, owners, slots):
    group_count = lax.axis_size(("pool", "ctx"))
    my_group = lax.axis_index(("pool", "ctx"))
    per_group = owners.size // group_count
    capacity = max(2, 2 * per_group // group_count) + 1

    def with_earlier(table, missing):
        grouped = table.reshape(-1, lax.axis_size("ctx"), per_group)
        earlier = jnp.pad(
            grouped[:, :-1, -NB_PER:], ((0, 0), (1, 0), (0, 0)), constant_values=missing
        )
        return jnp.concatenate([earlier, grouped], axis=2).reshape(group_count, -1)

    owner_table = with_earlier(owners, -1)
    slot_table = with_earlier(slots, 0)
    matched = (owner_table == my_group).astype(jnp.int32)
    order_rank = jnp.cumsum(matched, axis=1) - 1
    slot_index = jnp.arange(capacity, dtype=jnp.int32)
    picked = matched[:, None, :] * (order_rank[:, None, :] == slot_index[None, :, None]).astype(
        jnp.int32
    )
    source_rows = jnp.sum(picked * slot_table[:, None, :], axis=2).reshape(-1)
    outgoing = encoded[source_rows].reshape((group_count, capacity) + encoded.shape[1:])
    incoming = lax.all_to_all(outgoing, ("pool", "ctx"), split_axis=0, concat_axis=0, tiled=True)
    wanted = lax.dynamic_index_in_dim(owner_table, my_group, 0, keepdims=False)
    positions = jnp.arange(wanted.shape[0], dtype=jnp.int32)
    same_owner = (wanted[:, None] == wanted[None, :]).astype(jnp.int32)
    before_this = (positions[None, :] < positions[:, None]).astype(jnp.int32)
    arrival = jnp.maximum(wanted, 0) * capacity + jnp.sum(same_owner * before_this, axis=1)
    return incoming.reshape((group_count * capacity,) + encoded.shape[1:]), arrival, wanted


def neighbour_kernel(x_ref, w_ref, out_ref):
    out_ref[0] = jnp.dot(x_ref[...], w_ref[0], preferred_element_type=jnp.float32).astype(
        jnp.bfloat16
    )


def neighbour_kv(fetched, w_cross_kv):
    rows, depth = fetched.shape[0] * fetched.shape[1], fetched.shape[2]
    width = w_cross_kv.shape[2]
    tile = min(width, 256)
    steps = width // tile
    return pl.pallas_call(
        neighbour_kernel,
        grid=(2, steps),
        in_specs=[
            pl.BlockSpec((rows, depth), lambda c, j: (0, 0)),
            pl.BlockSpec((1, depth, tile), lambda c, j: (c, 0, j)),
        ],
        out_specs=pl.BlockSpec((1, rows, tile), lambda c, j: (c, 0, j)),
        out_shape=jax.ShapeDtypeStruct((2, rows, width), jnp.bfloat16),
        compiler_params=params(32, 2),
        cost_estimate=cost(4 * rows * depth * width, 4 * rows * width + 2 * rows * depth),
        name="neighbour_kv",
    )(in_hbm(fetched.reshape(rows, depth)), in_hbm(w_cross_kv))


def cross_kernel(q_ref, k_ref, v_ref, out_ref):
    rows = q_ref.shape[0]
    named = NB_PER * NB_TOK
    spans = rows // SPAN
    queries = pltpu.roll(q_ref[...].astype(jnp.float32), 1, 0).astype(jnp.bfloat16)

    parts = [queries[c * SPAN : (c + 1) * SPAN] for c in range(spans)] + [queries[:16]]
    scores = jnp.concatenate(
        [
            lax.dot_general(
                part,
                k_ref[0, c * named : (c + 1) * named, :],
                (((1,), (1,)), ((), ())),
                preferred_element_type=jnp.float32,
            )
            for c, part in enumerate(parts)
        ],
        axis=0,
    ) * (HEAD**-0.5 * LOG2E)
    weights = jnp.exp2(scores - jnp.max(scores, axis=1, keepdims=True))
    totals = jnp.sum(weights, axis=1, keepdims=True)
    weights = weights.astype(jnp.bfloat16)
    outs = [
        jnp.dot(
            weights[c * SPAN : c * SPAN + part.shape[0]],
            v_ref[0, c * named : (c + 1) * named, :],
            preferred_element_type=jnp.float32,
        )
        for c, part in enumerate(parts)
    ]
    whole = jnp.concatenate(outs, axis=0) / totals
    last, whole = whole[rows:], whole[:rows]
    last_row = jnp.broadcast_to(last[:1], whole.shape)
    row = lax.broadcasted_iota(jnp.int32, whole.shape, 0)
    whole = jnp.where(row == 0, last_row, whole)
    out_ref[...] = pltpu.roll(whole, rows - 1, 0).astype(jnp.bfloat16)


def cross_attention(queries, kv):
    rows, width = queries.shape
    heads = width // HEAD
    return pl.pallas_call(
        cross_kernel,
        grid=(heads,),
        in_specs=[
            pl.BlockSpec((rows, HEAD), lambda h: (0, h)),
            pl.BlockSpec((1, kv.shape[1], HEAD), lambda h: (0, 0, h)),
            pl.BlockSpec((1, kv.shape[1], HEAD), lambda h: (1, 0, h)),
        ],
        out_specs=pl.BlockSpec((rows, HEAD), lambda h: (0, h)),
        out_shape=jax.ShapeDtypeStruct((rows, width), jnp.bfloat16),
        compiler_params=params(24),
        cost_estimate=cost(1024 * rows * width, 4 * kv.shape[1] * width, 2 * rows * width),
        name="cross_attention",
    )(queries, kv, kv)


def per_device(
    tokens,
    norm_gain,
    cross_gain,
    w_query,
    w_key,
    w_value,
    w_out,
    w_cross_query,
    w_cross_kv,
    w_cross_out,
    encoded,
    owners,
    slots,
):
    own = tokens[0]
    normed = normalised(gather_blocks(own), norm_gain)
    neighbours = fetch_neighbours(encoded, owners, slots)
    attended, kv = self_attention(normed, w_query, w_key, w_value, neighbours, w_cross_kv)
    share = project_scattered(attended, w_out)
    residual = (own.astype(jnp.float32) + share).astype(jnp.bfloat16)
    cross_in = normalised(gather_blocks(residual), cross_gain)
    cross_queries = project(cross_in, w_cross_query, 0, w_cross_query.shape[1])
    crossed = cross_attention(cross_queries, kv)
    cross_part = project_scattered(crossed, w_cross_out)
    return (residual.astype(jnp.float32) + cross_part).astype(jnp.bfloat16)[None]


def solution(mesh):
    placed = (
        P("pool", "ctx", "mp"),
        P(),
        P(),
        P(None, "mp"),
        P(None, "mp"),
        P(None, "mp"),
        P("mp", None),
        P(None, "mp"),
        P(None, None, "mp"),
        P("mp", None),
        P(("pool", "ctx"), "mp", None),
        P(),
        P(),
    )
    return jax.shard_map(
        per_device, mesh=mesh, in_specs=placed, out_specs=P("pool", "ctx", "mp"), check_vma=False
    )
```
